32 devices in a mesh: wl: 4 (over y, x), tile: 8 (over z, core).
Axes of the slice: x: 2, y: 2, z: 4, core: 2. Of those that a mesh axis runs over, the one named last changes fastest.
Arguments:
- density: float32 [16, 1024], P('tile', 'wl'), may hold values from 0 to 1
- foot_index: int32 [4, 64, 4096], P(None, 'tile'), may hold values from 0 to 2047, as said below
- foot_weight: bfloat16 [4, 64, 4096], P(None, 'tile'), may hold values from 0.099609375 to 0.3984375
- source_fwd: float32 [8, 64, 4096], P('wl', 'tile'), may hold values from -6 to 6
- source_adj: float32 [8, 64, 4096], P('wl', 'tile'), may hold values from -6 to 6
- omega: float32 [8], P('wl'), may hold values from 0.2 to 1.5
Outputs:
- forward_field: float32 [8, 64, 4096], P('wl', 'tile')
- density_grad: float32 [16, 1024], P('tile', 'wl')
The draws below stay inside these ranges and needn't reach their ends.
Inputs may be any that keep to these rules, and one draw needn't show every extreme that they name: foot_index[f, x, y] = r * 1024 + c names coarse row r and column c of the strip of the tile holding row x, with r within one of (x mod 8) // 4 and c within two of y // 4; entry f = 0 is the cell's own block.
All inputs are finite; a program needn't handle non-finite values.
Results may differ from the reference program's by a relative error of at most 0.0003.
Values sent between devices are 32-bit elements; how exact they have to be, the bound alone decides.
A program may use at most 192 MiB of HBM per device.

```python
import math
import jax
import jax.numpy as jnp
from jax import lax

CX = 8
NY = 4096
FOOT = 4
ITERS = 4
NX = 64
BX = 16
BY = 1024
WL = 8


def draw_foot_index(key, part):
    key_row, key_col = jax.random.split(jax.random.fold_in(key, 11))
    row_shift = jax.random.randint(key_row, (FOOT, NX, NY), -1, 2)
    col_shift = jax.random.randint(key_col, (FOOT, NX, NY), -2, 3)
    entry = jnp.arange(FOOT, dtype=jnp.int32)[:, None, None]
    keep = (entry > 0).astype(jnp.int32)
    row_shift = row_shift * keep
    col_shift = col_shift * keep
    rows = jnp.arange(NX, dtype=jnp.int32)[None, :, None]
    cols = jnp.arange(NY, dtype=jnp.int32)[None, None, :]
    block_row = jnp.clip(rows % CX // 4 + row_shift, 0, CX // 4 - 1)
    block_col = jnp.clip(cols // 4 + col_shift, 0, NY // 4 - 1)
    return (block_row * (NY // 4) + block_col).astype(jnp.int32)


def block_levels(rng, shape, pieces, least, top_value):
    def one(dim, shards_of):
        steps = jax.random.uniform(jax.random.fold_in(jax.random.fold_in(rng, 6), dim), (shards_of,), jnp.float32, least / len(pieces), top_value / len(pieces))
        return jnp.repeat(jnp.exp(steps), shape[dim] // shards_of).reshape((-1,) + (1,) * (len(shape) - dim - 1))

    level = one(*pieces[0])
    for cut in pieces[1:]:
        level = level * one(*cut)
    return level


def gaussian(own_key, shape, width, reach, cuts=(), held_as=jnp.bfloat16):
    entries = width * jax.random.normal(own_key, shape, jnp.float32)
    if cuts:
        entries = entries * block_levels(own_key, shape, cuts, -0.22, 0.18)
    return jnp.clip(entries, -reach, reach).astype(held_as)


def setup_inputs(seed: int = 0) -> dict:
    key_of = jax.random.split(jax.random.key(seed), 7)
    return {
        "density": jnp.clip(1.0 * jax.random.uniform(key_of[0], (BX, BY), jnp.float32) ** block_levels(key_of[0], (BX, BY), ((0, 8), (1, 4)), -0.2, 0.2), 0.0, 1.0),
        "foot_index": draw_foot_index(jax.random.fold_in(key_of[6], 71), 0),
        "foot_weight": jnp.clip(0.099609375 + 0.29882812 * jax.random.uniform(key_of[2], (FOOT, NX, NY), jnp.float32) ** block_levels(key_of[2], (FOOT, NX, NY), ((1, 8),), -0.2, 0.2), 0.099609375, 0.3984375).astype(jnp.bfloat16),
        "source_fwd": gaussian(key_of[3], (WL, NX, NY), 1.0, 6.0, ((0, 4), (1, 8)), jnp.float32),
        "source_adj": gaussian(key_of[4], (WL, NX, NY), 1.0, 6.0, ((0, 4), (1, 8)), jnp.float32),
        "omega": jnp.clip(jnp.exp(math.log(1.5) - 2.014903 * jax.random.uniform(key_of[5], (WL,), jnp.float32) ** block_levels(key_of[5], (WL,), ((0, 4),), -0.2, 0.2)), 0.2, 1.5),
    }


time_step = 0.5
high_contrast = 4.0
drude_decay = 0.9
drude_gain = 0.5


def march(source, omega, density_cell, inverse):
    field_e = jnp.zeros_like(source)
    field_hx = jnp.zeros_like(source)
    field_hy = jnp.zeros_like(source)
    current = jnp.zeros_like(source)
    history = []
    for turn in range(ITERS):
        row_zero = jnp.zeros_like(source[:, :1, :])
        col_zero = jnp.zeros_like(source[:, :, :1])
        e_up = jnp.concatenate([field_e[:, 1:, :], row_zero], 1)
        e_right = jnp.concatenate([field_e[:, :, 1:], col_zero], 2)
        field_hx = field_hx - time_step * (e_right - field_e)
        field_hy = field_hy + time_step * (e_up - field_e)
        current = drude_decay * current + drude_gain * density_cell * field_e
        hy_down = jnp.concatenate([row_zero, field_hy[:, :-1, :]], 1)
        hx_left = jnp.concatenate([col_zero, field_hx[:, :, :-1]], 2)
        drive = jnp.sin(omega * (turn + 1.0))
        field_e = field_e + inverse * ((field_hy - hy_down) - (field_hx - hx_left) - current) + drive * source
        history.append(field_e)
    sense = jnp.zeros_like(source[0])
    for turn in range(ITERS):
        sense = sense + history[turn][1] * history[ITERS - 1 - turn][0]
    return field_e[0], sense


def reference(density, foot_index, foot_weight, source_fwd, source_adj, omega):
    rows = jnp.arange(NX, dtype=jnp.int32)
    offset = ((rows // CX) * ((CX // 4) * BY)).astype(jnp.int32)
    global_index = foot_index + offset[None, :, None]
    weights = foot_weight.astype(jnp.float32)
    flat = density.reshape(-1)
    density_cell = jnp.sum(weights * flat[global_index], axis=0)
    permittivity = 1.0 + high_contrast * density_cell
    inverse = time_step / permittivity

    def one(total, inputs):
        fwd, adj, freq = inputs
        final, sense = march(jnp.stack([fwd, adj]), freq, density_cell, inverse)
        return total + sense, final

    total, finals = lax.scan(one, jnp.zeros((NX, NY), jnp.float32), (source_fwd, source_adj, omega))
    values = (high_contrast / WL) * weights * total[None]
    grad = jax.ops.segment_sum(values.reshape(-1), global_index.reshape(-1), num_segments=BX * BY)
    return finals, grad.reshape(BX, BY)
```

```python
import functools

import jax
import jax.numpy as jnp
from jax import lax
from jax.experimental import pallas as pl
from jax.experimental.pallas import tpu as pltpu
from jax.sharding import PartitionSpec as P

ITERS = 4
CELLS = 4
REACH = 2
OFFSETS = 2 * REACH + 1
LANES = 128
WIDTH = CELLS * LANES

time_step = 0.5
high_contrast = 4.0
drude_decay = 0.9
drude_gain = 0.5

MESH = pl.DeviceIdType.MESH


def kernel(
    n_wl, n_tile, n_wave, cols, blocks, strip,
    dens_hbm, index_hbm, weight_hbm, fwd_hbm, adj_hbm, omega,
    field_hbm, grad_out,
    gathered, index, weight, src, table, density, inverse, matched, pool, drive,
    edge_src, field1, field2, field3, edge, curl, current, final, pooled,
    send_near, send_far, recv_near, recv_far, send_dens, recv_dens,
    part, part_in,
    local_sem, gather_send, gather_recv, halo_send, halo_recv, part_send, part_recv,
):
    wl = lax.axis_index("wl")
    tile = lax.axis_index("tile")
    piece = blocks // n_wl
    chunks = cols // WIDTH
    has_above, has_below = tile > 0, tile < n_tile - 1

    loads = [
        pltpu.make_async_copy(fwd_hbm, src.at[0], local_sem.at[0]),
        pltpu.make_async_copy(adj_hbm, src.at[1], local_sem.at[1]),
        pltpu.make_async_copy(dens_hbm, gathered.at[wl], local_sem.at[2]),
        pltpu.make_async_copy(index_hbm, index, local_sem.at[3]),
        pltpu.make_async_copy(weight_hbm, weight, local_sem.at[4]),
    ]
    for load in loads:
        load.start()

    barrier = pltpu.get_barrier_semaphore()
    peers = [lax.rem(wl + k, n_wl) for k in range(1, n_wl)]
    for peer in peers:
        pl.semaphore_signal(barrier, inc=1, device_id={"wl": peer}, device_id_type=MESH)

    @pl.when(has_above)
    def _():
        pl.semaphore_signal(barrier, inc=1, device_id={"tile": tile - 1}, device_id_type=MESH)

    @pl.when(has_below)
    def _():
        pl.semaphore_signal(barrier, inc=1, device_id={"tile": tile + 1}, device_id_type=MESH)

    loads[0].wait()
    loads[1].wait()
    for w in range(n_wave):
        for run in range(2):
            k = 2 * w + run
            send_near[0, 2 * k : 2 * k + 2, :] = src[run, w, 0:2, :]
            send_far[0, k : k + 1, :] = src[run, w, 2:3, :]
            send_near[1, 2 * k : 2 * k + 2, :] = src[run, w, 6:8, :]
            send_far[1, k : k + 1, :] = src[run, w, 5:6, :]

    @pl.when(tile == 0)
    def _():
        recv_near[1] = jnp.zeros_like(recv_near[1])
        recv_far[1] = jnp.zeros_like(recv_far[1])
        recv_dens[1] = jnp.zeros_like(recv_dens[1])

    @pl.when(tile == n_tile - 1)
    def _():
        recv_near[0] = jnp.zeros_like(recv_near[0])
        recv_far[0] = jnp.zeros_like(recv_far[0])
        recv_dens[0] = jnp.zeros_like(recv_dens[0])

    @pl.when(has_above & has_below)
    def _():
        pl.semaphore_wait(barrier, n_wl + 1)

    @pl.when(jnp.logical_not(has_above & has_below))
    def _():
        pl.semaphore_wait(barrier, n_wl)

    def gather_to(peer, slot):
        return pltpu.make_async_remote_copy(
            src_ref=dens_hbm, dst_ref=gathered.at[slot],
            send_sem=gather_send.at[peer], recv_sem=gather_recv.at[slot],
            device_id={"wl": peer}, device_id_type=MESH,
        )

    for peer in peers:
        gather_to(peer, wl).start()

    def halo(way, kind, source, target):
        other = tile - 1 if way == 0 else tile + 1
        return pltpu.make_async_remote_copy(
            src_ref=source.at[way], dst_ref=target.at[way],
            send_sem=halo_send.at[way, kind], recv_sem=halo_recv.at[way, kind],
            device_id={"tile": other}, device_id_type=MESH,
        )

    copies = ((send_near, recv_near), (send_far, recv_far), (send_dens, recv_dens))

    def sends(kinds, act):
        for way, there in ((0, has_above), (1, has_below)):
            @pl.when(there)
            def _():
                for kind in kinds:
                    act(halo(way, kind, *copies[kind]))

    def arrivals(kinds):
        for way, there in ((0, has_below), (1, has_above)):
            @pl.when(there)
            def _():
                for kind in kinds:
                    halo(way, kind, *copies[kind]).wait_recv()

    sends((0, 1), lambda copy: copy.start())

    row = lax.broadcasted_iota(jnp.int32, (8, LANES), 0)
    lane = lax.broadcasted_iota(jnp.int32, (8, LANES), 1)
    arg = jnp.zeros((8, LANES), jnp.float32)
    for w in range(n_wave):
        turn = (row - w * ITERS + 1).astype(jnp.float32)
        inside = (row >= w * ITERS) & (row < (w + 1) * ITERS)
        arg = jnp.where(inside, omega[w] * turn, arg)
    waves = jnp.sin(arg)
    for w in range(n_wave):
        for t in range(ITERS):
            k = w * ITERS + t
            drive[k] = jnp.broadcast_to(waves[k : k + 1, :], (8, LANES))
    cell = lax.broadcasted_iota(jnp.int32, (WIDTH, LANES), 0) // CELLS
    block = lax.broadcasted_iota(jnp.int32, (WIDTH, LANES), 1)
    pool[...] = (cell == block).astype(jnp.float32).astype(jnp.bfloat16)
    for field in (field1, field2, field3):
        for w in range(n_wave):
            for s in range(3):
                field[w, s, :, LANES + cols :] = jnp.zeros((8, LANES), jnp.float32)
    table[:, :, :LANES] = jnp.zeros((2, 8, LANES), jnp.float32)
    table[:, :, LANES + blocks :] = jnp.zeros((2, 8, LANES), jnp.float32)

    def spread(w, t):
        return jnp.concatenate([drive[w * ITERS + t]] * CELLS, axis=1)

    loads[2].wait()
    loads[3].wait()
    loads[4].wait()
    for peer in peers:
        gather_to(wl, peer).wait_recv()
    for i in range(n_wl):
        for r in range(2):
            table[r, :, LANES + piece * i : LANES + piece * (i + 1)] = jnp.broadcast_to(
                gathered[i, r : r + 1, :], (8, piece)
            )

    low = lane < LANES // 2
    keep_early = (lane >= 16) & (lane < 80)
    keep_late = (lane >= 48) & (lane < 112)

    def half(x):
        return pltpu.roll(x, LANES // 2, 1)

    def cell_density(g, carry):
        at = pl.multiple_of(g * LANES, LANES)
        before = [table[r, :, pl.ds(at, LANES)] for r in range(2)]
        here = [table[r, :, pl.ds(at + LANES, LANES)] for r in range(2)]
        after = [table[r, :, pl.ds(at + 2 * LANES, LANES)] for r in range(2)]
        turned = [half(before[0]), half(here[0]), half(after[0])]
        turned_row = half(here[1])
        tables = [
            jnp.where(keep_late, jnp.where(low, turned[0], turned[1]), jnp.where(low, here[1], before[1])),
            jnp.where(keep_early, here[0], turned_row),
            jnp.where(keep_late, here[0], turned_row),
            jnp.where(keep_early, jnp.where(low, turned[1], turned[2]), jnp.where(low, after[1], here[1])),
        ]
        for q in range(CELLS):
            start = pl.multiple_of(g * WIDTH + q * LANES, LANES)
            total = jnp.zeros((8, LANES), jnp.float32)
            for f in range(index.shape[0]):
                entry = index[f, :, pl.ds(start, LANES)]
                below = jnp.where(entry >= blocks, LANES // 2, 0)
                place = (entry + below + (LANES // 2 if q in (0, 3) else 0)) & (LANES - 1)
                value = jnp.take_along_axis(tables[q], place, axis=1, mode="promise_in_bounds")
                total = total + weight[f, :, pl.ds(start, LANES)].astype(jnp.float32) * value
            density[0, :, pl.ds(start, LANES)] = total
            inverse[0, :, pl.ds(start, LANES)] = time_step / (1.0 + high_contrast * total)
        return carry

    lax.fori_loop(0, chunks, cell_density, 0)
    send_dens[0] = density[0, 0:2, :]
    send_dens[1] = density[0, 6:8, :]
    sends((2,), lambda copy: copy.start())

    own = lax.broadcasted_iota(jnp.int32, (8, LANES), 1) // CELLS

    def weigh(g, carry):
        start = pl.multiple_of(g * LANES, LANES)
        base = own + g * (LANES // CELLS)
        shifts = [index[f, :, pl.ds(start, LANES)] - base for f in range(index.shape[0])]
        values = [weight[f, :, pl.ds(start, LANES)].astype(jnp.float32) for f in range(index.shape[0])]
        for r in range(2):
            for d in range(OFFSETS):
                target = r * blocks + d - REACH
                total = jnp.where(shifts[0] == target, values[0], 0.0)
                for f in range(1, index.shape[0]):
                    total = total + jnp.where(shifts[f] == target, values[f], 0.0)
                matched[r * OFFSETS + d, :, pl.ds(start, LANES)] = total
        return carry

    lax.fori_loop(0, cols // LANES, weigh, 0)

    arrivals((0, 1))
    for w in range(n_wave):
        for run in range(2):
            k = 2 * w + run
            edge_src[w, 2, 4 * run : 4 * run + 2, :] = recv_near[1, 2 * k : 2 * k + 2, :]
            edge_src[w, 2, 4 * run + 2 : 4 * run + 4, :] = recv_near[0, 2 * k : 2 * k + 2, :]
            edge[w, 2, 4 * run : 4 * run + 1, :] = recv_far[1, k : k + 1, :]
            edge[w, 2, 4 * run + 1 : 4 * run + 2, :] = src[run, w, 0:1, :]
            edge[w, 2, 4 * run + 2 : 4 * run + 3, :] = src[run, w, 7:8, :]
            edge[w, 2, 4 * run + 3 : 4 * run + 4, :] = recv_far[0, k : k + 1, :]

    first = tile == 0

    def rim(w, own_rows, halo_rows, where):
        for run in range(2):
            e = own_rows[run]
            above = jnp.where(first, e[0:1, :], halo_rows[4 * run + 1 : 4 * run + 2, :])
            edge[w, run, 0:1, where] = above
            edge[w, run, 7:8, where] = halo_rows[4 * run + 2 : 4 * run + 3, :]

    def start_fields(g, carry):
        where = pl.ds(pl.multiple_of(g * WIDTH, WIDTH), WIDTH)
        inner = pl.ds(pl.multiple_of(g * WIDTH + LANES, LANES), WIDTH)
        for w in range(n_wave):
            level = spread(w, 0)
            slabs = [level * src[0, w, :, where], level * src[1, w, :, where], level * edge_src[w, 2, :, where]]
            for s in range(3):
                field1[w, s, :, inner] = slabs[s]
            edge[w, 2, :, where] = level * edge[w, 2, :, where]
            rim(w, slabs, slabs[2], where)
        return carry

    lax.fori_loop(0, chunks, start_fields, 0)

    def mirror(field):
        for w in range(n_wave):
            for s in range(3):
                field[w, s, :, 0:LANES] = jnp.broadcast_to(field[w, s, :, LANES : LANES + 1], (8, LANES))

    mirror(field1)

    arrivals((2,))
    for k in range(2):
        density[1, 4 * k : 4 * k + 2, :] = recv_dens[1]
        density[1, 4 * k + 2 : 4 * k + 4, :] = recv_dens[0]

    wide_row = lax.broadcasted_iota(jnp.int32, (8, WIDTH), 0)
    beyond = (tile == n_tile - 1) & ((wide_row & 3) >= 2)
    odd = (wide_row & 1) == 1
    top = wide_row == 0
    bottom = wide_row == 7

    def invert(g, carry):
        where = pl.ds(pl.multiple_of(g * WIDTH, WIDTH), WIDTH)
        inverse[1, :, where] = jnp.where(beyond, 0.0, time_step / (1.0 + high_contrast * density[1, :, where]))
        return carry

    lax.fori_loop(0, chunks, invert, 0)

    def advance(t, old, g, w, s):
        where = pl.ds(pl.multiple_of(g * WIDTH, WIDTH), WIDTH)
        window = old[w, s, :, pl.ds(pl.multiple_of(g * WIDTH, WIDTH), WIDTH + 2 * LANES)]
        e = window[:, LANES : LANES + WIDTH]
        left = pltpu.roll(window, 1, 1)[:, LANES : LANES + WIDTH]
        right = pltpu.roll(window, WIDTH + 2 * LANES - 1, 1)[:, LANES : LANES + WIDTH]
        rows = edge[w, s, :, where]
        up = jnp.where(odd if s == 2 else bottom, rows, pltpu.roll(e, 7, 0))
        down = jnp.where((~odd) if s == 2 else top, rows, pltpu.roll(e, 1, 0))
        half_of = 1 if s == 2 else 0
        dens = density[half_of, :, where]
        c = time_step * (((up + down) + (left + right)) - 4.0 * e)
        j = (drude_gain * dens) * e
        if t > 1:
            c = c + curl[w, s, :, where]
            j = j + drude_decay * current[w, s, :, where]
        if t < ITERS - 1:
            curl[w, s, :, where] = c
            current[w, s, :, where] = j
        source = edge_src[w, 2, :, where] if s == 2 else src[s, w, :, where]
        return e + inverse[half_of, :, where] * (c - j) + spread(w, t) * source

    for t, old, new in ((1, field1, field2), (2, field2, field3)):
        def step(g, carry, t=t, old=old, new=new):
            where = pl.ds(pl.multiple_of(g * WIDTH, WIDTH), WIDTH)
            inner = pl.ds(pl.multiple_of(g * WIDTH + LANES, LANES), WIDTH)
            for w in range(n_wave):
                slabs = [advance(t, old, g, w, s) for s in range(3)]
                for s in range(3):
                    new[w, s, :, inner] = slabs[s]
                rim(w, slabs, slabs[2], where)
                for run in range(2):
                    edge[w, 2, 4 * run + 1 : 4 * run + 2, where] = slabs[run][0:1, :]
                    edge[w, 2, 4 * run + 2 : 4 * run + 3, where] = slabs[run][7:8, :]
            return carry

        lax.fori_loop(0, chunks, step, 0)
        mirror(new)

    def last(g, carry):
        where = pl.ds(pl.multiple_of(g * WIDTH, WIDTH), WIDTH)
        inner = pl.ds(pl.multiple_of(g * WIDTH + LANES, LANES), WIDTH)
        sense = jnp.zeros((8, WIDTH), jnp.float32)
        for w in range(n_wave):
            end_fwd = advance(ITERS - 1, field3, g, w, 0)
            end_adj = advance(ITERS - 1, field3, g, w, 1)
            final[w, :, where] = end_fwd
            sense = sense + (
                field1[w, 1, :, inner] * end_fwd
                + field2[w, 1, :, inner] * field3[w, 0, :, inner]
                + field3[w, 1, :, inner] * field2[w, 0, :, inner]
                + end_adj * field1[w, 0, :, inner]
            )
        terms = jnp.concatenate([matched[k, :, where] * sense for k in range(2 * OFFSETS)], axis=0)
        coarse = terms.astype(jnp.bfloat16)
        fine = (terms - coarse.astype(jnp.float32)).astype(jnp.bfloat16)
        sums = jnp.dot(coarse, pool[...], preferred_element_type=jnp.float32) + jnp.dot(
            fine, pool[...], preferred_element_type=jnp.float32
        )
        out = pl.ds(pl.multiple_of(g * LANES, LANES), LANES)
        for k in range(2 * OFFSETS):
            pooled[k, :, out] = sums[8 * k : 8 * k + 8, :]
        return carry

    lax.fori_loop(0, chunks, last, 0)
    store = pltpu.make_async_copy(final, field_hbm, local_sem.at[5])
    store.start()

    for r in range(2):
        total = pooled[r * OFFSETS + REACH]
        for d in range(-REACH, REACH + 1):
            if d:
                total = total + pltpu.roll(pooled[r * OFFSETS + REACH + d], d % blocks, 1)
        line = (high_contrast / (n_wl * n_wave)) * jnp.sum(total, axis=0, keepdims=True)
        for i in range(n_wl):
            part[i, r : r + 1, :] = line[:, piece * i : piece * (i + 1)]

    def part_to(peer, slot):
        return pltpu.make_async_remote_copy(
            src_ref=part.at[peer], dst_ref=part_in.at[slot],
            send_sem=part_send.at[peer], recv_sem=part_recv.at[slot],
            device_id={"wl": peer}, device_id_type=MESH,
        )

    for peer in peers:
        part_to(peer, wl).start()
    part_in[wl] = part[wl]
    for peer in peers:
        part_to(wl, peer).wait_recv()
    total = part_in[0]
    for i in range(1, n_wl):
        total = total + part_in[i]
    grad_out[...] = total

    for peer in peers:
        gather_to(peer, wl).wait_send()
        part_to(peer, wl).wait_send()
    sends((0, 1, 2), lambda copy: copy.wait_send())
    store.wait()


def shards(n_wl, n_tile, density, foot_index, foot_weight, source_fwd, source_adj, omega):
    n_wave, rows, cols = source_fwd.shape
    feet = foot_index.shape[0]
    strip, piece = density.shape
    blocks = piece * n_wl
    f32 = jnp.float32
    anywhere = pl.BlockSpec(memory_space=pl.ANY)
    padded = cols + 2 * LANES
    vmem = pltpu.VMEM
    dma = pltpu.SemaphoreType.DMA
    return pl.pallas_call(
        functools.partial(kernel, n_wl, n_tile, n_wave, cols, blocks, strip),
        out_shape=(
            jax.ShapeDtypeStruct(source_fwd.shape, f32),
            jax.ShapeDtypeStruct(density.shape, f32),
        ),
        in_specs=[anywhere] * 5 + [pl.BlockSpec(memory_space=pltpu.SMEM)],
        out_specs=(anywhere, pl.BlockSpec(memory_space=pltpu.VMEM)),
        scratch_shapes=[
            vmem((n_wl, strip, piece), f32),
            vmem((feet, rows, cols), jnp.int32),
            vmem((feet, rows, cols), jnp.bfloat16),
            vmem((2, n_wave, rows, cols), f32),
            vmem((2, 8, blocks + 2 * LANES), f32),
            vmem((2, rows, cols), f32),
            vmem((2, rows, cols), f32),
            vmem((2 * OFFSETS, rows, cols), f32),
            vmem((WIDTH, LANES), jnp.bfloat16),
            vmem((n_wave * ITERS, 8, LANES), f32),
            vmem((n_wave, 3, rows, cols), f32),
            vmem((n_wave, 3, rows, padded), f32),
            vmem((n_wave, 3, rows, padded), f32),
            vmem((n_wave, 3, rows, padded), f32),
            vmem((n_wave, 3, rows, cols), f32),
            vmem((n_wave, 3, rows, cols), f32),
            vmem((n_wave, 3, rows, cols), f32),
            vmem((n_wave, rows, cols), f32),
            vmem((2 * OFFSETS, rows, blocks), f32),
            vmem((2, 4 * n_wave, cols), f32),
            vmem((2, 2 * n_wave, cols), f32),
            vmem((2, 4 * n_wave, cols), f32),
            vmem((2, 2 * n_wave, cols), f32),
            vmem((2, 2, cols), f32),
            vmem((2, 2, cols), f32),
            vmem((n_wl, strip, piece), f32),
            vmem((n_wl, strip, piece), f32),
            dma((6,)),
            dma((n_wl,)),
            dma((n_wl,)),
            dma((2, 3)),
            dma((2, 3)),
            dma((n_wl,)),
            dma((n_wl,)),
        ],
        compiler_params=pltpu.CompilerParams(
            collective_id=0, has_side_effects=True, vmem_limit_bytes=48 * 1024 * 1024
        ),
        cost_estimate=pl.CostEstimate(flops=40_000_000, bytes_accessed=2_000_000, transcendentals=0),
    )(density, foot_index, foot_weight, source_fwd, source_adj, omega)


def solution(mesh):
    in_specs = (
        P("tile", "wl"),
        P(None, "tile", None),
        P(None, "tile", None),
        P("wl", "tile", None),
        P("wl", "tile", None),
        P("wl"),
    )
    out_specs = (P("wl", "tile", None), P("tile", "wl"))
    body = functools.partial(shards, mesh.shape["wl"], mesh.shape["tile"])
    return jax.shard_map(body, mesh=mesh, in_specs=in_specs, out_specs=out_specs, check_vma=False)
```

```python
import functools

import jax
import jax.numpy as jnp
from jax import lax
from jax.experimental import pallas as pl
from jax.experimental.pallas import tpu as pltpu
from jax.sharding import PartitionSpec as P

ITERS = 4
CELLS = 4
REACH = 2
OFFSETS = 2 * REACH + 1
LANES = 128
WIDTH = CELLS * LANES

time_step = 0.5
high_contrast = 4.0
drude_decay = 0.9
drude_gain = 0.5

MESH = pl.DeviceIdType.MESH


def kernel(
    n_wl, n_tile, n_wave, cols, blocks, strip,
    dens_hbm, index_hbm, weight_hbm, fwd_hbm, adj_hbm, omega,
    field_hbm, grad_out,
    gathered, index, weight, src, table, density, inverse, matched, pool, drive,
    edge_src, field1, field2, field3, edge, curl, current, final, pooled,
    send_near, send_far, recv_near, recv_far, send_dens, recv_dens,
    part, part_in,
    local_sem, gather_send, gather_recv, halo_send, halo_recv, part_send, part_recv,
):
    wl = lax.axis_index("wl")
    tile = lax.axis_index("tile")
    piece = blocks // n_wl
    chunks = cols // WIDTH
    has_above, has_below = tile > 0, tile < n_tile - 1

    loads = [
        pltpu.make_async_copy(fwd_hbm, src.at[0], local_sem.at[0]),
        pltpu.make_async_copy(adj_hbm, src.at[1], local_sem.at[1]),
        pltpu.make_async_copy(dens_hbm, gathered.at[wl], local_sem.at[2]),
        pltpu.make_async_copy(index_hbm, index, local_sem.at[3]),
        pltpu.make_async_copy(weight_hbm, weight, local_sem.at[4]),
    ]
    for load in loads:
        load.start()

    barrier = pltpu.get_barrier_semaphore()
    peers = [lax.rem(wl + k, n_wl) for k in range(1, n_wl)]
    for peer in peers:
        pl.semaphore_signal(barrier, inc=1, device_id={"wl": peer}, device_id_type=MESH)

    @pl.when(has_above)
    def _():
        pl.semaphore_signal(barrier, inc=1, device_id={"tile": tile - 1}, device_id_type=MESH)

    @pl.when(has_below)
    def _():
        pl.semaphore_signal(barrier, inc=1, device_id={"tile": tile + 1}, device_id_type=MESH)

    loads[0].wait()
    loads[1].wait()
    for w in range(n_wave):
        for run in range(2):
            k = 2 * w + run
            send_near[0, 2 * k : 2 * k + 2, :] = src[run, w, 0:2, :]
            send_far[0, k : k + 1, :] = src[run, w, 2:3, :]
            send_near[1, 2 * k : 2 * k + 2, :] = src[run, w, 6:8, :]
            send_far[1, k : k + 1, :] = src[run, w, 5:6, :]

    @pl.when(tile == 0)
    def _():
        recv_near[1] = jnp.zeros_like(recv_near[1])
        recv_far[1] = jnp.zeros_like(recv_far[1])
        recv_dens[1] = jnp.zeros_like(recv_dens[1])

    @pl.when(tile == n_tile - 1)
    def _():
        recv_near[0] = jnp.zeros_like(recv_near[0])
        recv_far[0] = jnp.zeros_like(recv_far[0])
        recv_dens[0] = jnp.zeros_like(recv_dens[0])

    @pl.when(has_above & has_below)
    def _():
        pl.semaphore_wait(barrier, n_wl + 1)

    @pl.when(jnp.logical_not(has_above & has_below))
    def _():
        pl.semaphore_wait(barrier, n_wl)

    def gather_to(peer, slot):
        return pltpu.make_async_remote_copy(
            src_ref=dens_hbm, dst_ref=gathered.at[slot],
            send_sem=gather_send.at[peer], recv_sem=gather_recv.at[slot],
            device_id={"wl": peer}, device_id_type=MESH,
        )

    for peer in peers:
        gather_to(peer, wl).start()

    def halo(way, kind, source, target):
        other = tile - 1 if way == 0 else tile + 1
        return pltpu.make_async_remote_copy(
            src_ref=source.at[way], dst_ref=target.at[way],
            send_sem=halo_send.at[way, kind], recv_sem=halo_recv.at[way, kind],
            device_id={"tile": other}, device_id_type=MESH,
        )

    copies = ((send_near, recv_near), (send_far, recv_far), (send_dens, recv_dens))

    def sends(kinds, act):
        for way, there in ((0, has_above), (1, has_below)):
            @pl.when(there)
            def _():
                for kind in kinds:
                    act(halo(way, kind, *copies[kind]))

    def arrivals(kinds):
        for way, there in ((0, has_below), (1, has_above)):
            @pl.when(there)
            def _():
                for kind in kinds:
                    halo(way, kind, *copies[kind]).wait_recv()

    sends((0, 1), lambda copy: copy.start())

    row = lax.broadcasted_iota(jnp.int32, (8, LANES), 0)
    lane = lax.broadcasted_iota(jnp.int32, (8, LANES), 1)
    arg = jnp.zeros((8, LANES), jnp.float32)
    for w in range(n_wave):
        turn = (row - w * ITERS + 1).astype(jnp.float32)
        inside = (row >= w * ITERS) & (row < (w + 1) * ITERS)
        arg = jnp.where(inside, omega[w] * turn, arg)
    waves = jnp.sin(arg)
    for w in range(n_wave):
        for t in range(ITERS):
            k = w * ITERS + t
            drive[k] = jnp.broadcast_to(waves[k : k + 1, :], (8, LANES))
    cell = lax.broadcasted_iota(jnp.int32, (WIDTH, LANES), 0) // CELLS
    block = lax.broadcasted_iota(jnp.int32, (WIDTH, LANES), 1)
    pool[...] = (cell == block).astype(jnp.float32).astype(jnp.bfloat16)
    for field in (field1, field2, field3):
        for w in range(n_wave):
            for s in range(3):
                field[w, s, :, LANES + cols :] = jnp.zeros((8, LANES), jnp.float32)
    table[:, :, :LANES] = jnp.zeros((2, 8, LANES), jnp.float32)
    table[:, :, LANES + blocks :] = jnp.zeros((2, 8, LANES), jnp.float32)

    def spread(w, t):
        return jnp.concatenate([drive[w * ITERS + t]] * CELLS, axis=1)

    loads[2].wait()
    loads[3].wait()
    loads[4].wait()
    for peer in peers:
        gather_to(wl, peer).wait_recv()
    for i in range(n_wl):
        for r in range(2):
            table[r, :, LANES + piece * i : LANES + piece * (i + 1)] = jnp.broadcast_to(
                gathered[i, r : r + 1, :], (8, piece)
            )

    low = lane < LANES // 2
    keep_early = (lane >= 16) & (lane < 80)
    keep_late = (lane >= 48) & (lane < 112)

    def half(x):
        return pltpu.roll(x, LANES // 2, 1)

    def cell_density(g, carry):
        at = pl.multiple_of(g * LANES, LANES)
        before = [table[r, :, pl.ds(at, LANES)] for r in range(2)]
        here = [table[r, :, pl.ds(at + LANES, LANES)] for r in range(2)]
        after = [table[r, :, pl.ds(at + 2 * LANES, LANES)] for r in range(2)]
        turned = [half(before[0]), half(here[0]), half(after[0])]
        turned_row = half(here[1])
        tables = [
            jnp.where(keep_late, jnp.where(low, turned[0], turned[1]), jnp.where(low, here[1], before[1])),
            jnp.where(keep_early, here[0], turned_row),
            jnp.where(keep_late, here[0], turned_row),
            jnp.where(keep_early, jnp.where(low, turned[1], turned[2]), jnp.where(low, after[1], here[1])),
        ]
        for q in range(CELLS):
            start = pl.multiple_of(g * WIDTH + q * LANES, LANES)
            total = jnp.zeros((8, LANES), jnp.float32)
            for f in range(index.shape[0]):
                entry = index[f, :, pl.ds(start, LANES)]
                below = jnp.where(entry >= blocks, LANES // 2, 0)
                place = (entry + below + (LANES // 2 if q in (0, 3) else 0)) & (LANES - 1)
                value = jnp.take_along_axis(tables[q], place, axis=1, mode="promise_in_bounds")
                total = total + weight[f, :, pl.ds(start, LANES)].astype(jnp.float32) * value
            density[0, :, pl.ds(start, LANES)] = total
            inverse[0, :, pl.ds(start, LANES)] = time_step / (1.0 + high_contrast * total)
        return carry

    lax.fori_loop(0, chunks, cell_density, 0)
    send_dens[0] = density[0, 0:2, :]
    send_dens[1] = density[0, 6:8, :]
    sends((2,), lambda copy: copy.start())

    own = lax.broadcasted_iota(jnp.int32, (8, LANES), 1) // CELLS

    def weigh(g, carry):
        start = pl.multiple_of(g * LANES, LANES)
        base = own + g * (LANES // CELLS)
        shifts = [index[f, :, pl.ds(start, LANES)] - base for f in range(index.shape[0])]
        values = [weight[f, :, pl.ds(start, LANES)].astype(jnp.float32) for f in range(index.shape[0])]
        for r in range(2):
            for d in range(OFFSETS):
                target = r * blocks + d - REACH
                total = jnp.where(shifts[0] == target, values[0], 0.0)
                for f in range(1, index.shape[0]):
                    total = total + jnp.where(shifts[f] == target, values[f], 0.0)
                matched[r * OFFSETS + d, :, pl.ds(start, LANES)] = total
        return carry

    lax.fori_loop(0, cols // LANES, weigh, 0)

    arrivals((0, 1))
    for w in range(n_wave):
        for run in range(2):
            k = 2 * w + run
            edge_src[w, 2, 4 * run : 4 * run + 2, :] = recv_near[1, 2 * k : 2 * k + 2, :]
            edge_src[w, 2, 4 * run + 2 : 4 * run + 4, :] = recv_near[0, 2 * k : 2 * k + 2, :]
            edge[w, 2, 4 * run : 4 * run + 1, :] = recv_far[1, k : k + 1, :]
            edge[w, 2, 4 * run + 1 : 4 * run + 2, :] = src[run, w, 0:1, :]
            edge[w, 2, 4 * run + 2 : 4 * run + 3, :] = src[run, w, 7:8, :]
            edge[w, 2, 4 * run + 3 : 4 * run + 4, :] = recv_far[0, k : k + 1, :]

    first = tile == 0

    def rim(w, own_rows, halo_rows, where):
        for run in range(2):
            e = own_rows[run]
            above = jnp.where(first, e[0:1, :], halo_rows[4 * run + 1 : 4 * run + 2, :])
            edge[w, run, 0:1, where] = above
            edge[w, run, 7:8, where] = halo_rows[4 * run + 2 : 4 * run + 3, :]

    def start_fields(g, carry):
        where = pl.ds(pl.multiple_of(g * WIDTH, WIDTH), WIDTH)
        inner = pl.ds(pl.multiple_of(g * WIDTH + LANES, LANES), WIDTH)
        for w in range(n_wave):
            level = spread(w, 0)
            slabs = [level * src[0, w, :, where], level * src[1, w, :, where], level * edge_src[w, 2, :, where]]
            for s in range(3):
                field1[w, s, :, inner] = slabs[s]
            edge[w, 2, :, where] = level * edge[w, 2, :, where]
            rim(w, slabs, slabs[2], where)
        return carry

    lax.fori_loop(0, chunks, start_fields, 0)

    def mirror(field):
        for w in range(n_wave):
            for s in range(3):
                field[w, s, :, 0:LANES] = jnp.broadcast_to(field[w, s, :, LANES : LANES + 1], (8, LANES))

    mirror(field1)

    arrivals((2,))
    for k in range(2):
        density[1, 4 * k : 4 * k + 2, :] = recv_dens[1]
        density[1, 4 * k + 2 : 4 * k + 4, :] = recv_dens[0]

    wide_row = lax.broadcasted_iota(jnp.int32, (8, WIDTH), 0)
    beyond = (tile == n_tile - 1) & ((wide_row & 3) >= 2)
    odd = (wide_row & 1) == 1
    top = wide_row == 0
    bottom = wide_row == 7

    def invert(g, carry):
        where = pl.ds(pl.multiple_of(g * WIDTH, WIDTH), WIDTH)
        inverse[1, :, where] = jnp.where(beyond, 0.0, time_step / (1.0 + high_contrast * density[1, :, where]))
        return carry

    lax.fori_loop(0, chunks, invert, 0)

    def advance(t, old, g, w, s):
        where = pl.ds(pl.multiple_of(g * WIDTH, WIDTH), WIDTH)
        window = old[w, s, :, pl.ds(pl.multiple_of(g * WIDTH, WIDTH), WIDTH + 2 * LANES)]
        e = window[:, LANES : LANES + WIDTH]
        left = pltpu.roll(window, 1, 1)[:, LANES : LANES + WIDTH]
        right = pltpu.roll(window, WIDTH + 2 * LANES - 1, 1)[:, LANES : LANES + WIDTH]
        rows = edge[w, s, :, where]
        up = jnp.where(odd if s == 2 else bottom, rows, pltpu.roll(e, 7, 0))
        down = jnp.where((~odd) if s == 2 else top, rows, pltpu.roll(e, 1, 0))
        half_of = 1 if s == 2 else 0
        dens = density[half_of, :, where]
        c = time_step * (((up + down) + (left + right)) - 4.0 * e)
        j = (drude_gain * dens) * e
        if t > 1:
            c = c + curl[w, s, :, where]
            j = j + drude_decay * current[w, s, :, where]
        if t < ITERS - 1:
            curl[w, s, :, where] = c
            current[w, s, :, where] = j
        source = edge_src[w, 2, :, where] if s == 2 else src[s, w, :, where]
        return e + inverse[half_of, :, where] * (c - j) + spread(w, t) * source

    for t, old, new in ((1, field1, field2), (2, field2, field3)):
        def step(g, carry, t=t, old=old, new=new):
            where = pl.ds(pl.multiple_of(g * WIDTH, WIDTH), WIDTH)
            inner = pl.ds(pl.multiple_of(g * WIDTH + LANES, LANES), WIDTH)
            for w in range(n_wave):
                slabs = [advance(t, old, g, w, s) for s in range(3)]
                for s in range(3):
                    new[w, s, :, inner] = slabs[s]
                rim(w, slabs, slabs[2], where)
                for run in range(2):
                    edge[w, 2, 4 * run + 1 : 4 * run + 2, where] = slabs[run][0:1, :]
                    edge[w, 2, 4 * run + 2 : 4 * run + 3, where] = slabs[run][7:8, :]
            return carry

        lax.fori_loop(0, chunks, step, 0)
        mirror(new)

    def last(g, carry):
        where = pl.ds(pl.multiple_of(g * WIDTH, WIDTH), WIDTH)
        inner = pl.ds(pl.multiple_of(g * WIDTH + LANES, LANES), WIDTH)
        sense = jnp.zeros((8, WIDTH), jnp.float32)
        for w in range(n_wave):
            end_fwd = advance(ITERS - 1, field3, g, w, 0)
            end_adj = advance(ITERS - 1, field3, g, w, 1)
            final[w, :, where] = end_fwd
            sense = sense + (
                field1[w, 1, :, inner] * end_fwd
                + field2[w, 1, :, inner] * field3[w, 0, :, inner]
                + field3[w, 1, :, inner] * field2[w, 0, :, inner]
                + end_adj * field1[w, 0, :, inner]
            )
        terms = jnp.concatenate([matched[k, :, where] * sense for k in range(2 * OFFSETS)], axis=0)
        coarse = terms.astype(jnp.bfloat16)
        fine = (terms - coarse.astype(jnp.float32)).astype(jnp.bfloat16)
        sums = jnp.dot(coarse, pool[...], preferred_element_type=jnp.float32) + jnp.dot(
            fine, pool[...], preferred_element_type=jnp.float32
        )
        out = pl.ds(pl.multiple_of(g * LANES, LANES), LANES)
        for k in range(2 * OFFSETS):
            pooled[k, :, out] = sums[8 * k : 8 * k + 8, :]
        return carry

    lax.fori_loop(0, chunks, last, 0)
    store = pltpu.make_async_copy(final, field_hbm, local_sem.at[5])
    store.start()

    for r in range(2):
        total = pooled[r * OFFSETS + REACH]
        for d in range(-REACH, REACH + 1):
            if d:
                total = total + pltpu.roll(pooled[r * OFFSETS + REACH + d], d % blocks, 1)
        line = (high_contrast / (n_wl * n_wave)) * jnp.sum(total, axis=0, keepdims=True)
        for i in range(n_wl):
            part[i, r : r + 1, :] = line[:, piece * i : piece * (i + 1)]

    def part_to(peer, slot):
        return pltpu.make_async_remote_copy(
            src_ref=part.at[peer], dst_ref=part_in.at[slot],
            send_sem=part_send.at[peer], recv_sem=part_recv.at[slot],
            device_id={"wl": peer}, device_id_type=MESH,
        )

    for peer in peers:
        part_to(peer, wl).start()
    part_in[wl] = part[wl]
    for peer in peers:
        part_to(wl, peer).wait_recv()
    total = part_in[0]
    for i in range(1, n_wl):
        total = total + part_in[i]
    grad_out[...] = total

    for peer in peers:
        gather_to(peer, wl).wait_send()
        part_to(peer, wl).wait_send()
    sends((0, 1, 2), lambda copy: copy.wait_send())
    store.wait()


def shards(n_wl, n_tile, density, foot_index, foot_weight, source_fwd, source_adj, omega):
    n_wave, rows, cols = source_fwd.shape
    feet = foot_index.shape[0]
    strip, piece = density.shape
    blocks = piece * n_wl
    f32 = jnp.float32
    anywhere = pl.BlockSpec(memory_space=pl.ANY)
    padded = cols + 2 * LANES
    vmem = pltpu.VMEM
    dma = pltpu.SemaphoreType.DMA
    return pl.pallas_call(
        functools.partial(kernel, n_wl, n_tile, n_wave, cols, blocks, strip),
        out_shape=(
            jax.ShapeDtypeStruct(source_fwd.shape, f32),
            jax.ShapeDtypeStruct(density.shape, f32),
        ),
        in_specs=[anywhere] * 5 + [pl.BlockSpec(memory_space=pltpu.SMEM)],
        out_specs=(anywhere, pl.BlockSpec(memory_space=pltpu.VMEM)),
        scratch_shapes=[
            vmem((n_wl, strip, piece), f32),
            vmem((feet, rows, cols), jnp.int32),
            vmem((feet, rows, cols), jnp.bfloat16),
            vmem((2, n_wave, rows, cols), f32),
            vmem((2, 8, blocks + 2 * LANES), f32),
            vmem((2, rows, cols), f32),
            vmem((2, rows, cols), f32),
            vmem((2 * OFFSETS, rows, cols), f32),
            vmem((WIDTH, LANES), jnp.bfloat16),
            vmem((n_wave * ITERS, 8, LANES), f32),
            vmem((n_wave, 3, rows, cols), f32),
            vmem((n_wave, 3, rows, padded), f32),
            vmem((n_wave, 3, rows, padded), f32),
            vmem((n_wave, 3, rows, padded), f32),
            vmem((n_wave, 3, rows, cols), f32),
            vmem((n_wave, 3, rows, cols), f32),
            vmem((n_wave, 3, rows, cols), f32),
            vmem((n_wave, rows, cols), f32),
            vmem((2 * OFFSETS, rows, blocks), f32),
            vmem((2, 4 * n_wave, cols), f32),
            vmem((2, 2 * n_wave, cols), f32),
            vmem((2, 4 * n_wave, cols), f32),
            vmem((2, 2 * n_wave, cols), f32),
            vmem((2, 2, cols), f32),
            vmem((2, 2, cols), f32),
            vmem((n_wl, strip, piece), f32),
            vmem((n_wl, strip, piece), f32),
            dma((6,)),
            dma((n_wl,)),
            dma((n_wl,)),
            dma((2, 3)),
            dma((2, 3)),
            dma((n_wl,)),
            dma((n_wl,)),
        ],
        compiler_params=pltpu.CompilerParams(
            collective_id=0, has_side_effects=True
        ),
        cost_estimate=pl.CostEstimate(flops=40_000_000, bytes_accessed=2_000_000, transcendentals=0),
    )(density, foot_index, foot_weight, source_fwd, source_adj, omega)


def solution(mesh):
    in_specs = (
        P("tile", "wl"),
        P(None, "tile", None),
        P(None, "tile", None),
        P("wl", "tile", None),
        P("wl", "tile", None),
        P("wl"),
    )
    out_specs = (P("wl", "tile", None), P("tile", "wl"))
    body = functools.partial(shards, mesh.shape["wl"], mesh.shape["tile"])
    return jax.shard_map(body, mesh=mesh, in_specs=in_specs, out_specs=out_specs, check_vma=False)
```

```python
import functools

import jax
import jax.numpy as jnp
from jax import lax
from jax.experimental import pallas as pl
from jax.experimental.pallas import tpu as pltpu
from jax.sharding import PartitionSpec as P

ITERS = 4
CELLS = 4
REACH = 2
OFFSETS = 2 * REACH + 1
LANES = 128
WIDTH = CELLS * LANES

time_step = 0.5
high_contrast = 4.0
drude_decay = 0.9
drude_gain = 0.5

MESH = pl.DeviceIdType.MESH


def kernel(
    n_wl, n_tile, n_wave, cols, blocks, strip,
    dens_hbm, index_hbm, weight_hbm, fwd_hbm, adj_hbm, omega,
    field_hbm, grad_out,
    gathered, index, weight, src, table, density, inverse, matched, pool, drive,
    edge_src, field1, field2, field3, edge, curl, current, final, pooled,
    send_near, send_far, recv_near, recv_far, send_dens, recv_dens,
    part, part_in,
    local_sem, gather_send, gather_recv, halo_send, halo_recv, part_send, part_recv,
):
    wl = lax.axis_index("wl")
    tile = lax.axis_index("tile")
    piece = blocks // n_wl
    chunks = cols // WIDTH
    has_above, has_below = tile > 0, tile < n_tile - 1

    loads = [
        pltpu.make_async_copy(fwd_hbm, src.at[0], local_sem.at[0]),
        pltpu.make_async_copy(adj_hbm, src.at[1], local_sem.at[1]),
        pltpu.make_async_copy(dens_hbm, gathered.at[wl], local_sem.at[2]),
        pltpu.make_async_copy(index_hbm, index, local_sem.at[3]),
        pltpu.make_async_copy(weight_hbm, weight, local_sem.at[4]),
    ]
    for load in loads:
        load.start()

    barrier = pltpu.get_barrier_semaphore()
    peers = [lax.rem(wl + k, n_wl) for k in range(1, n_wl)]
    for peer in peers:
        pl.semaphore_signal(barrier, inc=1, device_id={"wl": peer}, device_id_type=MESH)

    @pl.when(has_above)
    def _():
        pl.semaphore_signal(barrier, inc=1, device_id={"tile": tile - 1}, device_id_type=MESH)

    @pl.when(has_below)
    def _():
        pl.semaphore_signal(barrier, inc=1, device_id={"tile": tile + 1}, device_id_type=MESH)

    loads[0].wait()
    loads[1].wait()
    for w in range(n_wave):
        for run in range(2):
            k = 2 * w + run
            send_near[0, 2 * k : 2 * k + 2, :] = src[run, w, 0:2, :]
            send_far[0, k : k + 1, :] = src[run, w, 2:3, :]
            send_near[1, 2 * k : 2 * k + 2, :] = src[run, w, 6:8, :]
            send_far[1, k : k + 1, :] = src[run, w, 5:6, :]

    @pl.when(tile == 0)
    def _():
        recv_near[1] = jnp.zeros_like(recv_near[1])
        recv_far[1] = jnp.zeros_like(recv_far[1])
        recv_dens[1] = jnp.zeros_like(recv_dens[1])

    @pl.when(tile == n_tile - 1)
    def _():
        recv_near[0] = jnp.zeros_like(recv_near[0])
        recv_far[0] = jnp.zeros_like(recv_far[0])
        recv_dens[0] = jnp.zeros_like(recv_dens[0])

    @pl.when(has_above & has_below)
    def _():
        pl.semaphore_wait(barrier, n_wl + 1)

    @pl.when(jnp.logical_not(has_above & has_below))
    def _():
        pl.semaphore_wait(barrier, n_wl)

    def gather_to(peer, slot):
        return pltpu.make_async_remote_copy(
            src_ref=dens_hbm, dst_ref=gathered.at[slot],
            send_sem=gather_send.at[peer], recv_sem=gather_recv.at[slot],
            device_id={"wl": peer}, device_id_type=MESH,
        )

    for peer in peers:
        gather_to(peer, wl).start()

    def halo(way, kind, source, target):
        other = tile - 1 if way == 0 else tile + 1
        return pltpu.make_async_remote_copy(
            src_ref=source.at[way], dst_ref=target.at[way],
            send_sem=halo_send.at[way, kind], recv_sem=halo_recv.at[way, kind],
            device_id={"tile": other}, device_id_type=MESH,
        )

    copies = ((send_near, recv_near), (send_far, recv_far), (send_dens, recv_dens))

    def sends(kinds, act):
        for way, there in ((0, has_above), (1, has_below)):
            @pl.when(there)
            def _():
                for kind in kinds:
                    act(halo(way, kind, *copies[kind]))

    def arrivals(kinds):
        for way, there in ((0, has_below), (1, has_above)):
            @pl.when(there)
            def _():
                for kind in kinds:
                    halo(way, kind, *copies[kind]).wait_recv()

    sends((0, 1), lambda copy: copy.start())

    row = lax.broadcasted_iota(jnp.int32, (8, LANES), 0)
    lane = lax.broadcasted_iota(jnp.int32, (8, LANES), 1)
    arg = jnp.zeros((8, LANES), jnp.float32)
    for w in range(n_wave):
        turn = (row - w * ITERS + 1).astype(jnp.float32)
        inside = (row >= w * ITERS) & (row < (w + 1) * ITERS)
        arg = jnp.where(inside, omega[w] * turn, arg)
    waves = jnp.sin(arg)
    for w in range(n_wave):
        for t in range(ITERS):
            k = w * ITERS + t
            drive[k] = jnp.broadcast_to(waves[k : k + 1, :], (8, LANES))
    cell = lax.broadcasted_iota(jnp.int32, (WIDTH, LANES), 0) // CELLS
    block = lax.broadcasted_iota(jnp.int32, (WIDTH, LANES), 1)
    pool[...] = (cell == block).astype(jnp.float32).astype(jnp.bfloat16)
    for field in (field1, field2, field3):
        for w in range(n_wave):
            for s in range(3):
                field[w, s, :, LANES + cols :] = jnp.zeros((8, LANES), jnp.float32)
    table[:, :, :LANES] = jnp.zeros((2, 8, LANES), jnp.float32)
    table[:, :, LANES + blocks :] = jnp.zeros((2, 8, LANES), jnp.float32)

    def spread(w, t):
        return jnp.concatenate([drive[w * ITERS + t]] * CELLS, axis=1)

    loads[3].wait()
    loads[4].wait()
    own = lax.broadcasted_iota(jnp.int32, (8, LANES), 1) // CELLS

    def weigh(g, carry):
        start = pl.multiple_of(g * LANES, LANES)
        base = own + g * (LANES // CELLS)
        shifts = [index[f, :, pl.ds(start, LANES)] - base for f in range(index.shape[0])]
        values = [weight[f, :, pl.ds(start, LANES)].astype(jnp.float32) for f in range(index.shape[0])]
        for r in range(2):
            for d in range(OFFSETS):
                target = r * blocks + d - REACH
                total = jnp.where(shifts[0] == target, values[0], 0.0)
                for f in range(1, index.shape[0]):
                    total = total + jnp.where(shifts[f] == target, values[f], 0.0)
                matched[r * OFFSETS + d, :, pl.ds(start, LANES)] = total
        return carry

    lax.fori_loop(0, cols // LANES, weigh, 0, unroll=2)

    loads[2].wait()
    for peer in peers:
        gather_to(wl, peer).wait_recv()
    for i in range(n_wl):
        for r in range(2):
            table[r, :, LANES + piece * i : LANES + piece * (i + 1)] = jnp.broadcast_to(
                gathered[i, r : r + 1, :], (8, piece)
            )

    low = lane < LANES // 2
    keep_early = (lane >= 16) & (lane < 80)
    keep_late = (lane >= 48) & (lane < 112)

    def half(x):
        return pltpu.roll(x, LANES // 2, 1)

    def cell_density(g, carry):
        at = pl.multiple_of(g * LANES, LANES)
        before = [table[r, :, pl.ds(at, LANES)] for r in range(2)]
        here = [table[r, :, pl.ds(at + LANES, LANES)] for r in range(2)]
        after = [table[r, :, pl.ds(at + 2 * LANES, LANES)] for r in range(2)]
        turned = [half(before[0]), half(here[0]), half(after[0])]
        turned_row = half(here[1])
        tables = [
            jnp.where(keep_late, jnp.where(low, turned[0], turned[1]), jnp.where(low, here[1], before[1])),
            jnp.where(keep_early, here[0], turned_row),
            jnp.where(keep_late, here[0], turned_row),
            jnp.where(keep_early, jnp.where(low, turned[1], turned[2]), jnp.where(low, after[1], here[1])),
        ]
        for q in range(CELLS):
            start = pl.multiple_of(g * WIDTH + q * LANES, LANES)
            total = jnp.zeros((8, LANES), jnp.float32)
            for f in range(index.shape[0]):
                entry = index[f, :, pl.ds(start, LANES)]
                below = jnp.where(entry >= blocks, LANES // 2, 0)
                place = (entry + below + (LANES // 2 if q in (0, 3) else 0)) & (LANES - 1)
                value = jnp.take_along_axis(tables[q], place, axis=1, mode="promise_in_bounds")
                total = total + weight[f, :, pl.ds(start, LANES)].astype(jnp.float32) * value
            density[0, :, pl.ds(start, LANES)] = total
            inverse[0, :, pl.ds(start, LANES)] = time_step / (1.0 + high_contrast * total)
        return carry

    lax.fori_loop(0, chunks, cell_density, 0)
    send_dens[0] = density[0, 0:2, :]
    send_dens[1] = density[0, 6:8, :]
    sends((2,), lambda copy: copy.start())

    arrivals((0, 1))
    for w in range(n_wave):
        for run in range(2):
            k = 2 * w + run
            edge_src[w, 2, 4 * run : 4 * run + 2, :] = recv_near[1, 2 * k : 2 * k + 2, :]
            edge_src[w, 2, 4 * run + 2 : 4 * run + 4, :] = recv_near[0, 2 * k : 2 * k + 2, :]
            edge[w, 2, 4 * run : 4 * run + 1, :] = recv_far[1, k : k + 1, :]
            edge[w, 2, 4 * run + 1 : 4 * run + 2, :] = src[run, w, 0:1, :]
            edge[w, 2, 4 * run + 2 : 4 * run + 3, :] = src[run, w, 7:8, :]
            edge[w, 2, 4 * run + 3 : 4 * run + 4, :] = recv_far[0, k : k + 1, :]

    first = tile == 0

    def rim(w, own_rows, halo_rows, where):
        for run in range(2):
            e = own_rows[run]
            above = jnp.where(first, e[0:1, :], halo_rows[4 * run + 1 : 4 * run + 2, :])
            edge[w, run, 0:1, where] = above
            edge[w, run, 7:8, where] = halo_rows[4 * run + 2 : 4 * run + 3, :]

    def start_fields(g, carry):
        where = pl.ds(pl.multiple_of(g * WIDTH, WIDTH), WIDTH)
        inner = pl.ds(pl.multiple_of(g * WIDTH + LANES, LANES), WIDTH)
        for w in range(n_wave):
            level = spread(w, 0)
            slabs = [level * src[0, w, :, where], level * src[1, w, :, where], level * edge_src[w, 2, :, where]]
            for s in range(3):
                field1[w, s, :, inner] = slabs[s]
            edge[w, 2, :, where] = level * edge[w, 2, :, where]
            rim(w, slabs, slabs[2], where)
        return carry

    lax.fori_loop(0, chunks, start_fields, 0)

    def mirror(field):
        for w in range(n_wave):
            for s in range(3):
                field[w, s, :, 0:LANES] = jnp.broadcast_to(field[w, s, :, LANES : LANES + 1], (8, LANES))

    mirror(field1)

    arrivals((2,))
    for k in range(2):
        density[1, 4 * k : 4 * k + 2, :] = recv_dens[1]
        density[1, 4 * k + 2 : 4 * k + 4, :] = recv_dens[0]

    wide_row = lax.broadcasted_iota(jnp.int32, (8, WIDTH), 0)
    beyond = (tile == n_tile - 1) & ((wide_row & 3) >= 2)
    odd = (wide_row & 1) == 1
    top = wide_row == 0
    bottom = wide_row == 7

    def invert(g, carry):
        where = pl.ds(pl.multiple_of(g * WIDTH, WIDTH), WIDTH)
        inverse[1, :, where] = jnp.where(beyond, 0.0, time_step / (1.0 + high_contrast * density[1, :, where]))
        return carry

    lax.fori_loop(0, chunks, invert, 0)

    def advance(t, old, g, w, s):
        where = pl.ds(pl.multiple_of(g * WIDTH, WIDTH), WIDTH)
        window = old[w, s, :, pl.ds(pl.multiple_of(g * WIDTH, WIDTH), WIDTH + 2 * LANES)]
        e = window[:, LANES : LANES + WIDTH]
        left = pltpu.roll(window, 1, 1)[:, LANES : LANES + WIDTH]
        right = pltpu.roll(window, WIDTH + 2 * LANES - 1, 1)[:, LANES : LANES + WIDTH]
        rows = edge[w, s, :, where]
        up = jnp.where(odd if s == 2 else bottom, rows, pltpu.roll(e, 7, 0))
        down = jnp.where((~odd) if s == 2 else top, rows, pltpu.roll(e, 1, 0))
        half_of = 1 if s == 2 else 0
        dens = density[half_of, :, where]
        c = time_step * (((up + down) + (left + right)) - 4.0 * e)
        j = (drude_gain * dens) * e
        if t > 1:
            c = c + curl[w, s, :, where]
            j = j + drude_decay * current[w, s, :, where]
        if t < ITERS - 1:
            curl[w, s, :, where] = c
            current[w, s, :, where] = j
        source = edge_src[w, 2, :, where] if s == 2 else src[s, w, :, where]
        return e + inverse[half_of, :, where] * (c - j) + spread(w, t) * source

    for t, old, new in ((1, field1, field2), (2, field2, field3)):
        def step(g, carry, t=t, old=old, new=new):
            where = pl.ds(pl.multiple_of(g * WIDTH, WIDTH), WIDTH)
            inner = pl.ds(pl.multiple_of(g * WIDTH + LANES, LANES), WIDTH)
            for w in range(n_wave):
                slabs = [advance(t, old, g, w, s) for s in range(3)]
                for s in range(3):
                    new[w, s, :, inner] = slabs[s]
                rim(w, slabs, slabs[2], where)
                for run in range(2):
                    edge[w, 2, 4 * run + 1 : 4 * run + 2, where] = slabs[run][0:1, :]
                    edge[w, 2, 4 * run + 2 : 4 * run + 3, where] = slabs[run][7:8, :]
            return carry

        lax.fori_loop(0, chunks, step, 0)
        mirror(new)

    def last(g, carry):
        where = pl.ds(pl.multiple_of(g * WIDTH, WIDTH), WIDTH)
        inner = pl.ds(pl.multiple_of(g * WIDTH + LANES, LANES), WIDTH)
        sense = jnp.zeros((8, WIDTH), jnp.float32)
        for w in range(n_wave):
            end_fwd = advance(ITERS - 1, field3, g, w, 0)
            end_adj = advance(ITERS - 1, field3, g, w, 1)
            final[w, :, where] = end_fwd
            sense = sense + (
                field1[w, 1, :, inner] * end_fwd
                + field2[w, 1, :, inner] * field3[w, 0, :, inner]
                + field3[w, 1, :, inner] * field2[w, 0, :, inner]
                + end_adj * field1[w, 0, :, inner]
            )
        terms = jnp.concatenate([matched[k, :, where] * sense for k in range(2 * OFFSETS)], axis=0)
        coarse = terms.astype(jnp.bfloat16)
        fine = (terms - coarse.astype(jnp.float32)).astype(jnp.bfloat16)
        sums = jnp.dot(coarse, pool[...], preferred_element_type=jnp.float32) + jnp.dot(
            fine, pool[...], preferred_element_type=jnp.float32
        )
        out = pl.ds(pl.multiple_of(g * LANES, LANES), LANES)
        for k in range(2 * OFFSETS):
            pooled[k, :, out] = sums[8 * k : 8 * k + 8, :]
        return carry

    lax.fori_loop(0, chunks, last, 0)
    store = pltpu.make_async_copy(final, field_hbm, local_sem.at[5])
    store.start()

    for r in range(2):
        total = pooled[r * OFFSETS + REACH]
        for d in range(-REACH, REACH + 1):
            if d:
                total = total + pltpu.roll(pooled[r * OFFSETS + REACH + d], d % blocks, 1)
        line = (high_contrast / (n_wl * n_wave)) * jnp.sum(total, axis=0, keepdims=True)
        for i in range(n_wl):
            part[i, r : r + 1, :] = line[:, piece * i : piece * (i + 1)]

    def part_to(peer, slot):
        return pltpu.make_async_remote_copy(
            src_ref=part.at[peer], dst_ref=part_in.at[slot],
            send_sem=part_send.at[peer], recv_sem=part_recv.at[slot],
            device_id={"wl": peer}, device_id_type=MESH,
        )

    for peer in peers:
        part_to(peer, wl).start()
    part_in[wl] = part[wl]
    for peer in peers:
        part_to(wl, peer).wait_recv()
    total = part_in[0]
    for i in range(1, n_wl):
        total = total + part_in[i]
    grad_out[...] = total

    for peer in peers:
        gather_to(peer, wl).wait_send()
        part_to(peer, wl).wait_send()
    sends((0, 1, 2), lambda copy: copy.wait_send())
    store.wait()


def shards(n_wl, n_tile, density, foot_index, foot_weight, source_fwd, source_adj, omega):
    n_wave, rows, cols = source_fwd.shape
    feet = foot_index.shape[0]
    strip, piece = density.shape
    blocks = piece * n_wl
    f32 = jnp.float32
    anywhere = pl.BlockSpec(memory_space=pl.ANY)
    padded = cols + 2 * LANES
    vmem = pltpu.VMEM
    dma = pltpu.SemaphoreType.DMA
    return pl.pallas_call(
        functools.partial(kernel, n_wl, n_tile, n_wave, cols, blocks, strip),
        out_shape=(
            jax.ShapeDtypeStruct(source_fwd.shape, f32),
            jax.ShapeDtypeStruct(density.shape, f32),
        ),
        in_specs=[anywhere] * 5 + [pl.BlockSpec(memory_space=pltpu.SMEM)],
        out_specs=(anywhere, pl.BlockSpec(memory_space=pltpu.VMEM)),
        scratch_shapes=[
            vmem((n_wl, strip, piece), f32),
            vmem((feet, rows, cols), jnp.int32),
            vmem((feet, rows, cols), jnp.bfloat16),
            vmem((2, n_wave, rows, cols), f32),
            vmem((2, 8, blocks + 2 * LANES), f32),
            vmem((2, rows, cols), f32),
            vmem((2, rows, cols), f32),
            vmem((2 * OFFSETS, rows, cols), f32),
            vmem((WIDTH, LANES), jnp.bfloat16),
            vmem((n_wave * ITERS, 8, LANES), f32),
            vmem((n_wave, 3, rows, cols), f32),
            vmem((n_wave, 3, rows, padded), f32),
            vmem((n_wave, 3, rows, padded), f32),
            vmem((n_wave, 3, rows, padded), f32),
            vmem((n_wave, 3, rows, cols), f32),
            vmem((n_wave, 3, rows, cols), f32),
            vmem((n_wave, 3, rows, cols), f32),
            vmem((n_wave, rows, cols), f32),
            vmem((2 * OFFSETS, rows, blocks), f32),
            vmem((2, 4 * n_wave, cols), f32),
            vmem((2, 2 * n_wave, cols), f32),
            vmem((2, 4 * n_wave, cols), f32),
            vmem((2, 2 * n_wave, cols), f32),
            vmem((2, 2, cols), f32),
            vmem((2, 2, cols), f32),
            vmem((n_wl, strip, piece), f32),
            vmem((n_wl, strip, piece), f32),
            dma((6,)),
            dma((n_wl,)),
            dma((n_wl,)),
            dma((2, 3)),
            dma((2, 3)),
            dma((n_wl,)),
            dma((n_wl,)),
        ],
        compiler_params=pltpu.CompilerParams(
            collective_id=0, has_side_effects=True
        ),
        cost_estimate=pl.CostEstimate(flops=40_000_000, bytes_accessed=2_000_000, transcendentals=0),
    )(density, foot_index, foot_weight, source_fwd, source_adj, omega)


def solution(mesh):
    in_specs = (
        P("tile", "wl"),
        P(None, "tile", None),
        P(None, "tile", None),
        P("wl", "tile", None),
        P("wl", "tile", None),
        P("wl"),
    )
    out_specs = (P("wl", "tile", None), P("tile", "wl"))
    body = functools.partial(shards, mesh.shape["wl"], mesh.shape["tile"])
    return jax.shard_map(body, mesh=mesh, in_specs=in_specs, out_specs=out_specs, check_vma=False)
```

```python
import functools

import jax
import jax.numpy as jnp
from jax import lax
from jax.experimental import pallas as pl
from jax.experimental.pallas import tpu as pltpu
from jax.sharding import PartitionSpec as P

ITERS = 4
CELLS = 4
REACH = 2
OFFSETS = 2 * REACH + 1
LANES = 128
WIDTH = CELLS * LANES

time_step = 0.5
high_contrast = 4.0
drude_decay = 0.9
drude_gain = 0.5

MESH = pl.DeviceIdType.MESH


def kernel(
    n_wl, n_tile, n_wave, cols, blocks, strip,
    dens_hbm, index_hbm, weight_hbm, fwd_hbm, adj_hbm, omega,
    field_hbm, grad_out,
    gathered, index, weight, src, table, density, inverse, matched, pool, drive,
    edge_src, field1, field2, field3, edge, curl, current, final, pooled,
    send_near, send_far, recv_near, recv_far, send_dens, recv_dens,
    part, part_in,
    local_sem, gather_send, gather_recv, halo_send, halo_recv, part_send, part_recv,
):
    wl = lax.axis_index("wl")
    tile = lax.axis_index("tile")
    piece = blocks // n_wl
    chunks = cols // WIDTH
    has_above, has_below = tile > 0, tile < n_tile - 1

    loads = [
        pltpu.make_async_copy(fwd_hbm, src.at[0], local_sem.at[0]),
        pltpu.make_async_copy(adj_hbm, src.at[1], local_sem.at[1]),
        pltpu.make_async_copy(dens_hbm, gathered.at[wl], local_sem.at[2]),
        pltpu.make_async_copy(index_hbm, index, local_sem.at[3]),
        pltpu.make_async_copy(weight_hbm, weight, local_sem.at[4]),
    ]
    for load in loads:
        load.start()

    barrier = pltpu.get_barrier_semaphore()
    peers = [lax.rem(wl + k, n_wl) for k in range(1, n_wl)]
    for peer in peers:
        pl.semaphore_signal(barrier, inc=1, device_id={"wl": peer}, device_id_type=MESH)

    @pl.when(has_above)
    def _():
        pl.semaphore_signal(barrier, inc=1, device_id={"tile": tile - 1}, device_id_type=MESH)

    @pl.when(has_below)
    def _():
        pl.semaphore_signal(barrier, inc=1, device_id={"tile": tile + 1}, device_id_type=MESH)

    loads[0].wait()
    loads[1].wait()
    for w in range(n_wave):
        for run in range(2):
            k = 2 * w + run
            send_near[0, 2 * k : 2 * k + 2, :] = src[run, w, 0:2, :]
            send_far[0, k : k + 1, :] = src[run, w, 2:3, :]
            send_near[1, 2 * k : 2 * k + 2, :] = src[run, w, 6:8, :]
            send_far[1, k : k + 1, :] = src[run, w, 5:6, :]

    @pl.when(tile == 0)
    def _():
        recv_near[1] = jnp.zeros_like(recv_near[1])
        recv_far[1] = jnp.zeros_like(recv_far[1])
        recv_dens[1] = jnp.zeros_like(recv_dens[1])

    @pl.when(tile == n_tile - 1)
    def _():
        recv_near[0] = jnp.zeros_like(recv_near[0])
        recv_far[0] = jnp.zeros_like(recv_far[0])
        recv_dens[0] = jnp.zeros_like(recv_dens[0])

    @pl.when(has_above & has_below)
    def _():
        pl.semaphore_wait(barrier, n_wl + 1)

    @pl.when(jnp.logical_not(has_above & has_below))
    def _():
        pl.semaphore_wait(barrier, n_wl)

    def gather_to(peer, slot):
        return pltpu.make_async_remote_copy(
            src_ref=dens_hbm, dst_ref=gathered.at[slot],
            send_sem=gather_send.at[peer], recv_sem=gather_recv.at[slot],
            device_id={"wl": peer}, device_id_type=MESH,
        )

    for peer in peers:
        gather_to(peer, wl).start()

    def halo(way, kind, source, target):
        other = tile - 1 if way == 0 else tile + 1
        return pltpu.make_async_remote_copy(
            src_ref=source.at[way], dst_ref=target.at[way],
            send_sem=halo_send.at[way, kind], recv_sem=halo_recv.at[way, kind],
            device_id={"tile": other}, device_id_type=MESH,
        )

    copies = ((send_near, recv_near), (send_far, recv_far), (send_dens, recv_dens))

    def sends(kinds, act):
        for way, there in ((0, has_above), (1, has_below)):
            @pl.when(there)
            def _():
                for kind in kinds:
                    act(halo(way, kind, *copies[kind]))

    def arrivals(kinds):
        for way, there in ((0, has_below), (1, has_above)):
            @pl.when(there)
            def _():
                for kind in kinds:
                    halo(way, kind, *copies[kind]).wait_recv()

    sends((0, 1), lambda copy: copy.start())

    row = lax.broadcasted_iota(jnp.int32, (8, LANES), 0)
    lane = lax.broadcasted_iota(jnp.int32, (8, LANES), 1)
    arg = jnp.zeros((8, LANES), jnp.float32)
    for w in range(n_wave):
        turn = (row - w * ITERS + 1).astype(jnp.float32)
        inside = (row >= w * ITERS) & (row < (w + 1) * ITERS)
        arg = jnp.where(inside, omega[w] * turn, arg)
    waves = jnp.sin(arg)
    for w in range(n_wave):
        for t in range(ITERS):
            k = w * ITERS + t
            drive[k] = jnp.broadcast_to(waves[k : k + 1, :], (8, LANES))
    cell = lax.broadcasted_iota(jnp.int32, (WIDTH, LANES), 0) // CELLS
    block = lax.broadcasted_iota(jnp.int32, (WIDTH, LANES), 1)
    pool[...] = (cell == block).astype(jnp.float32).astype(jnp.bfloat16)
    for field in (field1, field2, field3):
        for w in range(n_wave):
            for s in range(3):
                field[w, s, :, LANES + cols :] = jnp.zeros((8, LANES), jnp.float32)
    table[:, :, :LANES] = jnp.zeros((2, 8, LANES), jnp.float32)
    table[:, :, LANES + blocks :] = jnp.zeros((2, 8, LANES), jnp.float32)

    def spread(w, t):
        return jnp.concatenate([drive[w * ITERS + t]] * CELLS, axis=1)

    loads[3].wait()
    loads[4].wait()
    own = lax.broadcasted_iota(jnp.int32, (8, LANES), 1) // CELLS

    def weigh(g, carry):
        start = pl.multiple_of(g * LANES, LANES)
        base = own + g * (LANES // CELLS)
        shifts = [index[f, :, pl.ds(start, LANES)] - base for f in range(index.shape[0])]
        values = [weight[f, :, pl.ds(start, LANES)].astype(jnp.float32) for f in range(index.shape[0])]
        for r in range(2):
            for d in range(OFFSETS):
                target = r * blocks + d - REACH
                total = jnp.where(shifts[0] == target, values[0], 0.0)
                for f in range(1, index.shape[0]):
                    total = total + jnp.where(shifts[f] == target, values[f], 0.0)
                matched[r * OFFSETS + d, :, pl.ds(start, LANES)] = total
        return carry

    lax.fori_loop(0, cols // LANES, weigh, 0, unroll=2)

    loads[2].wait()
    for peer in peers:
        gather_to(wl, peer).wait_recv()
    for i in range(n_wl):
        for r in range(2):
            table[r, :, LANES + piece * i : LANES + piece * (i + 1)] = jnp.broadcast_to(
                gathered[i, r : r + 1, :], (8, piece)
            )

    low = lane < LANES // 2
    keep_early = (lane >= 16) & (lane < 80)
    keep_late = (lane >= 48) & (lane < 112)

    def half(x):
        return pltpu.roll(x, LANES // 2, 1)

    def cell_density(g, carry):
        at = pl.multiple_of(g * LANES, LANES)
        before = [table[r, :, pl.ds(at, LANES)] for r in range(2)]
        here = [table[r, :, pl.ds(at + LANES, LANES)] for r in range(2)]
        after = [table[r, :, pl.ds(at + 2 * LANES, LANES)] for r in range(2)]
        turned = [half(before[0]), half(here[0]), half(after[0])]
        turned_row = half(here[1])
        tables = [
            jnp.where(keep_late, jnp.where(low, turned[0], turned[1]), jnp.where(low, here[1], before[1])),
            jnp.where(keep_early, here[0], turned_row),
            jnp.where(keep_late, here[0], turned_row),
            jnp.where(keep_early, jnp.where(low, turned[1], turned[2]), jnp.where(low, after[1], here[1])),
        ]
        for q in range(CELLS):
            start = pl.multiple_of(g * WIDTH + q * LANES, LANES)
            total = jnp.zeros((8, LANES), jnp.float32)
            for f in range(index.shape[0]):
                entry = index[f, :, pl.ds(start, LANES)]
                below = jnp.where(entry >= blocks, LANES // 2, 0)
                place = (entry + below + (LANES // 2 if q in (0, 3) else 0)) & (LANES - 1)
                value = jnp.take_along_axis(tables[q], place, axis=1, mode="promise_in_bounds")
                total = total + weight[f, :, pl.ds(start, LANES)].astype(jnp.float32) * value
            density[0, :, pl.ds(start, LANES)] = total
            inverse[0, :, pl.ds(start, LANES)] = time_step / (1.0 + high_contrast * total)
        return carry

    lax.fori_loop(0, chunks, cell_density, 0, unroll=2)
    send_dens[0] = density[0, 0:2, :]
    send_dens[1] = density[0, 6:8, :]
    sends((2,), lambda copy: copy.start())

    arrivals((0, 1))
    for w in range(n_wave):
        for run in range(2):
            k = 2 * w + run
            edge_src[w, 2, 4 * run : 4 * run + 2, :] = recv_near[1, 2 * k : 2 * k + 2, :]
            edge_src[w, 2, 4 * run + 2 : 4 * run + 4, :] = recv_near[0, 2 * k : 2 * k + 2, :]
            edge[w, 2, 4 * run : 4 * run + 1, :] = recv_far[1, k : k + 1, :]
            edge[w, 2, 4 * run + 1 : 4 * run + 2, :] = src[run, w, 0:1, :]
            edge[w, 2, 4 * run + 2 : 4 * run + 3, :] = src[run, w, 7:8, :]
            edge[w, 2, 4 * run + 3 : 4 * run + 4, :] = recv_far[0, k : k + 1, :]

    first = tile == 0

    def rim(w, own_rows, halo_rows, where):
        for run in range(2):
            e = own_rows[run]
            above = jnp.where(first, e[0:1, :], halo_rows[4 * run + 1 : 4 * run + 2, :])
            edge[w, run, 0:1, where] = above
            edge[w, run, 7:8, where] = halo_rows[4 * run + 2 : 4 * run + 3, :]

    def start_fields(g, carry):
        where = pl.ds(pl.multiple_of(g * WIDTH, WIDTH), WIDTH)
        inner = pl.ds(pl.multiple_of(g * WIDTH + LANES, LANES), WIDTH)
        for w in range(n_wave):
            level = spread(w, 0)
            slabs = [level * src[0, w, :, where], level * src[1, w, :, where], level * edge_src[w, 2, :, where]]
            for s in range(3):
                field1[w, s, :, inner] = slabs[s]
            edge[w, 2, :, where] = level * edge[w, 2, :, where]
            rim(w, slabs, slabs[2], where)
        return carry

    lax.fori_loop(0, chunks, start_fields, 0, unroll=2)

    def mirror(field):
        for w in range(n_wave):
            for s in range(3):
                field[w, s, :, 0:LANES] = jnp.broadcast_to(field[w, s, :, LANES : LANES + 1], (8, LANES))

    mirror(field1)

    arrivals((2,))
    for k in range(2):
        density[1, 4 * k : 4 * k + 2, :] = recv_dens[1]
        density[1, 4 * k + 2 : 4 * k + 4, :] = recv_dens[0]

    wide_row = lax.broadcasted_iota(jnp.int32, (8, WIDTH), 0)
    beyond = (tile == n_tile - 1) & ((wide_row & 3) >= 2)
    odd = (wide_row & 1) == 1
    top = wide_row == 0
    bottom = wide_row == 7

    def invert(g, carry):
        where = pl.ds(pl.multiple_of(g * WIDTH, WIDTH), WIDTH)
        inverse[1, :, where] = jnp.where(beyond, 0.0, time_step / (1.0 + high_contrast * density[1, :, where]))
        return carry

    lax.fori_loop(0, chunks, invert, 0, unroll=4)

    def advance(t, old, g, w, s):
        where = pl.ds(pl.multiple_of(g * WIDTH, WIDTH), WIDTH)
        window = old[w, s, :, pl.ds(pl.multiple_of(g * WIDTH, WIDTH), WIDTH + 2 * LANES)]
        e = window[:, LANES : LANES + WIDTH]
        left = pltpu.roll(window, 1, 1)[:, LANES : LANES + WIDTH]
        right = pltpu.roll(window, WIDTH + 2 * LANES - 1, 1)[:, LANES : LANES + WIDTH]
        rows = edge[w, s, :, where]
        up = jnp.where(odd if s == 2 else bottom, rows, pltpu.roll(e, 7, 0))
        down = jnp.where((~odd) if s == 2 else top, rows, pltpu.roll(e, 1, 0))
        half_of = 1 if s == 2 else 0
        dens = density[half_of, :, where]
        c = time_step * (((up + down) + (left + right)) - 4.0 * e)
        j = (drude_gain * dens) * e
        if t > 1:
            c = c + curl[w, s, :, where]
            j = j + drude_decay * current[w, s, :, where]
        if t < ITERS - 1:
            curl[w, s, :, where] = c
            current[w, s, :, where] = j
        source = edge_src[w, 2, :, where] if s == 2 else src[s, w, :, where]
        return e + inverse[half_of, :, where] * (c - j) + spread(w, t) * source

    for t, old, new in ((1, field1, field2), (2, field2, field3)):
        def step(g, carry, t=t, old=old, new=new):
            where = pl.ds(pl.multiple_of(g * WIDTH, WIDTH), WIDTH)
            inner = pl.ds(pl.multiple_of(g * WIDTH + LANES, LANES), WIDTH)
            for w in range(n_wave):
                slabs = [advance(t, old, g, w, s) for s in range(3)]
                for s in range(3):
                    new[w, s, :, inner] = slabs[s]
                rim(w, slabs, slabs[2], where)
                for run in range(2):
                    edge[w, 2, 4 * run + 1 : 4 * run + 2, where] = slabs[run][0:1, :]
                    edge[w, 2, 4 * run + 2 : 4 * run + 3, where] = slabs[run][7:8, :]
            return carry

        lax.fori_loop(0, chunks, step, 0, unroll=2)
        mirror(new)

    def last(g, carry):
        where = pl.ds(pl.multiple_of(g * WIDTH, WIDTH), WIDTH)
        inner = pl.ds(pl.multiple_of(g * WIDTH + LANES, LANES), WIDTH)
        sense = jnp.zeros((8, WIDTH), jnp.float32)
        for w in range(n_wave):
            end_fwd = advance(ITERS - 1, field3, g, w, 0)
            end_adj = advance(ITERS - 1, field3, g, w, 1)
            final[w, :, where] = end_fwd
            sense = sense + (
                field1[w, 1, :, inner] * end_fwd
                + field2[w, 1, :, inner] * field3[w, 0, :, inner]
                + field3[w, 1, :, inner] * field2[w, 0, :, inner]
                + end_adj * field1[w, 0, :, inner]
            )
        terms = jnp.concatenate([matched[k, :, where] * sense for k in range(2 * OFFSETS)], axis=0)
        coarse = terms.astype(jnp.bfloat16)
        fine = (terms - coarse.astype(jnp.float32)).astype(jnp.bfloat16)
        sums = jnp.dot(coarse, pool[...], preferred_element_type=jnp.float32) + jnp.dot(
            fine, pool[...], preferred_element_type=jnp.float32
        )
        out = pl.ds(pl.multiple_of(g * LANES, LANES), LANES)
        for k in range(2 * OFFSETS):
            pooled[k, :, out] = sums[8 * k : 8 * k + 8, :]
        return carry

    lax.fori_loop(0, chunks, last, 0, unroll=2)
    store = pltpu.make_async_copy(final, field_hbm, local_sem.at[5])
    store.start()

    for r in range(2):
        total = pooled[r * OFFSETS + REACH]
        for d in range(-REACH, REACH + 1):
            if d:
                total = total + pltpu.roll(pooled[r * OFFSETS + REACH + d], d % blocks, 1)
        line = (high_contrast / (n_wl * n_wave)) * jnp.sum(total, axis=0, keepdims=True)
        for i in range(n_wl):
            part[i, r : r + 1, :] = line[:, piece * i : piece * (i + 1)]

    def part_to(peer, slot):
        return pltpu.make_async_remote_copy(
            src_ref=part.at[peer], dst_ref=part_in.at[slot],
            send_sem=part_send.at[peer], recv_sem=part_recv.at[slot],
            device_id={"wl": peer}, device_id_type=MESH,
        )

    for peer in peers:
        part_to(peer, wl).start()
    part_in[wl] = part[wl]
    for peer in peers:
        part_to(wl, peer).wait_recv()
    total = part_in[0]
    for i in range(1, n_wl):
        total = total + part_in[i]
    grad_out[...] = total

    for peer in peers:
        gather_to(peer, wl).wait_send()
        part_to(peer, wl).wait_send()
    sends((0, 1, 2), lambda copy: copy.wait_send())
    store.wait()


def shards(n_wl, n_tile, density, foot_index, foot_weight, source_fwd, source_adj, omega):
    n_wave, rows, cols = source_fwd.shape
    feet = foot_index.shape[0]
    strip, piece = density.shape
    blocks = piece * n_wl
    f32 = jnp.float32
    anywhere = pl.BlockSpec(memory_space=pl.ANY)
    padded = cols + 2 * LANES
    vmem = pltpu.VMEM
    dma = pltpu.SemaphoreType.DMA
    return pl.pallas_call(
        functools.partial(kernel, n_wl, n_tile, n_wave, cols, blocks, strip),
        out_shape=(
            jax.ShapeDtypeStruct(source_fwd.shape, f32),
            jax.ShapeDtypeStruct(density.shape, f32),
        ),
        in_specs=[anywhere] * 5 + [pl.BlockSpec(memory_space=pltpu.SMEM)],
        out_specs=(anywhere, pl.BlockSpec(memory_space=pltpu.VMEM)),
        scratch_shapes=[
            vmem((n_wl, strip, piece), f32),
            vmem((feet, rows, cols), jnp.int32),
            vmem((feet, rows, cols), jnp.bfloat16),
            vmem((2, n_wave, rows, cols), f32),
            vmem((2, 8, blocks + 2 * LANES), f32),
            vmem((2, rows, cols), f32),
            vmem((2, rows, cols), f32),
            vmem((2 * OFFSETS, rows, cols), f32),
            vmem((WIDTH, LANES), jnp.bfloat16),
            vmem((n_wave * ITERS, 8, LANES), f32),
            vmem((n_wave, 3, rows, cols), f32),
            vmem((n_wave, 3, rows, padded), f32),
            vmem((n_wave, 3, rows, padded), f32),
            vmem((n_wave, 3, rows, padded), f32),
            vmem((n_wave, 3, rows, cols), f32),
            vmem((n_wave, 3, rows, cols), f32),
            vmem((n_wave, 3, rows, cols), f32),
            vmem((n_wave, rows, cols), f32),
            vmem((2 * OFFSETS, rows, blocks), f32),
            vmem((2, 4 * n_wave, cols), f32),
            vmem((2, 2 * n_wave, cols), f32),
            vmem((2, 4 * n_wave, cols), f32),
            vmem((2, 2 * n_wave, cols), f32),
            vmem((2, 2, cols), f32),
            vmem((2, 2, cols), f32),
            vmem((n_wl, strip, piece), f32),
            vmem((n_wl, strip, piece), f32),
            dma((6,)),
            dma((n_wl,)),
            dma((n_wl,)),
            dma((2, 3)),
            dma((2, 3)),
            dma((n_wl,)),
            dma((n_wl,)),
        ],
        compiler_params=pltpu.CompilerParams(
            collective_id=0, has_side_effects=True
        ),
        cost_estimate=pl.CostEstimate(flops=40_000_000, bytes_accessed=2_000_000, transcendentals=0),
    )(density, foot_index, foot_weight, source_fwd, source_adj, omega)


def solution(mesh):
    in_specs = (
        P("tile", "wl"),
        P(None, "tile", None),
        P(None, "tile", None),
        P("wl", "tile", None),
        P("wl", "tile", None),
        P("wl"),
    )
    out_specs = (P("wl", "tile", None), P("tile", "wl"))
    body = functools.partial(shards, mesh.shape["wl"], mesh.shape["tile"])
    return jax.shard_map(body, mesh=mesh, in_specs=in_specs, out_specs=out_specs, check_vma=False)
```
